128 devices in a mesh: dom: 64 (over z, y, x), row: 2 (over core).
Axes of the slice: x: 4, y: 4, z: 4, core: 2. Of those that a mesh axis runs over, the one named last changes fastest.
Arguments:
- right_side: float32 [64, 1024, 512], P('dom', 'row'), may hold values from -6 to 6
- lower_blocks: bfloat16 [64, 6, 1024, 1024], P('dom', None, 'row'), may hold values from -0.15625 to 0.15625
- upper_blocks: bfloat16 [64, 6, 1024, 1024], P('dom', None, 'row'), may hold values from -0.15625 to 0.15625
- final_blocks: bfloat16 [64, 1024, 1024], P('dom', 'row'), may hold values from -0.0234375 to 0.0234375
Outputs:
- solution: float32 [64, 1024, 512], P('dom', 'row')
The draws below stay inside these ranges and needn't reach their ends.
All inputs are finite; a program needn't handle non-finite values.
Results may differ from the reference program's by a relative error of at most 0.008.
Values may be sent and summed in bfloat16 or wider, within the bound.
A program may use at most 64 MiB of HBM per device.

```python
import jax
import jax.numpy as jnp

W = 1024
RHS = 512
SLICES = 64
LEVELS = 6


def block_levels(own_key, dims, split, least, high):
    gain, own = 1.0, jax.random.fold_in(own_key, 6)
    for dim, blocks in split:
        steps = jnp.exp(jax.random.uniform(jax.random.fold_in(own, dim), (blocks,), jnp.float32, least / len(split), high / len(split)))
        gain = gain * jnp.repeat(steps, dims[dim] // blocks).reshape([-1 if axis == dim else 1 for axis in range(len(dims))])
    return gain


def noise(stream_key, extent, width, bound, shards=(), kind=jnp.bfloat16):
    values = width * jax.random.normal(stream_key, extent, jnp.float32)
    if shards:
        values = values * block_levels(stream_key, extent, shards, -0.22, 0.18)
    return jnp.clip(values, -bound, bound).astype(kind)


def setup_inputs(seed: int = 0) -> dict:
    key_list = jax.random.split(jax.random.key(seed), 5)
    return {
        "right_side": noise(key_list[0], (SLICES, W, RHS), 1.0, 6.0, ((0, 64), (1, 2)), jnp.float32),
        "lower_blocks": noise(key_list[1], (SLICES, LEVELS, W, W), (W * 25 // 16) ** -0.5, 0.15625, ((0, 64), (2, 2))),
        "upper_blocks": noise(key_list[2], (SLICES, LEVELS, W, W), (W * 25 // 16) ** -0.5, 0.15625, ((0, 64), (2, 2))),
        "final_blocks": noise(key_list[3], (SLICES, W, W), (W * 2 ** LEVELS) ** -0.5, 0.0234375, ((0, 64), (1, 2))),
    }


def shifted(values, distance):
    zeros = jnp.zeros((distance,) + values.shape[1:], values.dtype)
    from_low = jnp.concatenate([zeros, values[:-distance]], 0)
    from_high = jnp.concatenate([values[distance:], zeros], 0)
    return from_low, from_high


def reference(right_side, lower_blocks, upper_blocks, final_blocks):
    current = right_side
    for level_index in range(LEVELS):
        distance = 2 ** level_index
        rounded = current.astype(jnp.bfloat16)
        from_low, from_high = shifted(rounded, distance)
        lower_term = jnp.einsum("pij,pjm->pim", lower_blocks[:, level_index].astype(jnp.float32), from_low.astype(jnp.float32))
        upper_term = jnp.einsum("pij,pjm->pim", upper_blocks[:, level_index].astype(jnp.float32), from_high.astype(jnp.float32))
        current = current + lower_term + upper_term
    final_state = current.astype(jnp.bfloat16)
    return jnp.einsum("pij,pjm->pim", final_blocks.astype(jnp.float32), final_state.astype(jnp.float32))
```

```python
import functools

import jax
import jax.numpy as jnp
from jax import lax
from jax.experimental import pallas as pl
from jax.experimental.pallas import tpu as pltpu
from jax.sharding import PartitionSpec as P

MESH = pl.DeviceIdType.MESH
CHUNKS = 4
LAG = 1
EARLY = True


def kernel(slices, levels, rs_ref, lo_ref, up_ref, fin_ref, out_ref,
           lo_v, up_v, fin_v, cur, snd, low, high, gat,
           load_sem, s_sem, r_sem, fs_sem, fr_sem, gs_sem, gr_sem):
    half, cols = snd.shape[2], snd.shape[3]
    chunks = snd.shape[1]
    me, row = lax.axis_index("dom"), lax.axis_index("row")
    sib = 1 - row
    mine = pl.ds(pl.multiple_of(row * half, half), half)

    loads = []
    for l in range(levels):
        loads.append((
            pltpu.make_async_copy(lo_ref.at[0, l], lo_v.at[l], load_sem.at[0, l]),
            pltpu.make_async_copy(up_ref.at[0, l], up_v.at[l], load_sem.at[1, l])))
    loads.append((pltpu.make_async_copy(fin_ref.at[0], fin_v, load_sem.at[0, levels]),))
    for group in loads:
        for copy in group:
            copy.start()

    barrier = pltpu.get_barrier_semaphore()
    pl.semaphore_signal(barrier, inc=1, device_id=(me, sib), device_id_type=MESH)
    count = 1
    for l in range(levels):
        d = 2 ** l
        for ok, peer in ((me >= d, me - d), (me + d < slices, me + d)):
            count = count + ok.astype(jnp.int32)

            @pl.when(ok)
            def _():
                pl.semaphore_signal(barrier, inc=1, device_id=(peer, row), device_id_type=MESH)
    pl.semaphore_wait(barrier, count)

    def sides(l):
        d = 2 ** l
        return ((me + d < slices, me + d, me >= d, low), (me >= d, me - d, me + d < slices, high))

    def send(c, l, side, peer, buf):
        return pltpu.make_async_remote_copy(
            snd.at[l, c], buf.at[l, c, mine], s_sem.at[side, l, c], r_sem.at[side, l, c], (peer, row), MESH)

    def forward(c, l, side, buf):
        return pltpu.make_async_remote_copy(
            buf.at[l, c, mine], buf.at[l, c, mine], fs_sem.at[side, l, c], fr_sem.at[side, l, c], (me, sib), MESH)

    def share(c):
        return pltpu.make_async_remote_copy(
            gat.at[c, mine], gat.at[c, mine], gs_sem.at[c], gr_sem.at[c], (me, sib), MESH)

    def do_send(c, l):
        lanes = slice(c * cols, (c + 1) * cols)
        source = rs_ref[0, :, lanes] if l == 0 else cur[:, lanes]
        if l == levels:
            gat[c, mine] = source.astype(jnp.bfloat16)
            share(c).start()
            return
        snd[l, c] = source.astype(jnp.bfloat16)
        for side, (to, peer, _, buf) in enumerate(sides(l)):
            @pl.when(to)
            def _():
                send(c, l, side, peer, buf).start()

    def do_forward(c, l):
        if l == levels:
            return
        for side, (_, peer, got, buf) in enumerate(sides(l)):
            @pl.when(got)
            def _():
                send(c, l, side, peer, buf).wait_recv()
                forward(c, l, side, buf).start()

    def do_math(c, l):
        lanes = slice(c * cols, (c + 1) * cols)
        if l == levels:
            share(c).wait_recv()
            if c == 0:
                loads[l][0].wait()
            out_ref[0, :, lanes] = jnp.dot(fin_v[...], gat[c], preferred_element_type=jnp.float32)
            return
        if c == 0:
            for copy in loads[l]:
                copy.wait()
        if l == 0:
            cur[:, lanes] = rs_ref[0, :, lanes]
        for side, (_, _, got, buf) in enumerate(sides(l)):
            weights = (lo_v, up_v)[side]

            @pl.when(got)
            def _():
                forward(c, l, side, buf).wait_recv()
                cur[:, lanes] += jnp.dot(weights[l], buf[l, c], preferred_element_type=jnp.float32)

    if EARLY:
        for c in range(chunks):
            do_send(c, 0)
    for step in range(levels + 1 + LAG * (chunks - 1)):
        active = [(c, step - LAG * c) for c in range(chunks) if 0 <= step - LAG * c <= levels]
        if not EARLY:
            for c, l in active:
                if l == 0:
                    do_send(c, 0)
        for c, l in active:
            do_forward(c, l)
        for c, l in active:
            do_math(c, l)
            if l < levels:
                do_send(c, l + 1)

    for c in range(chunks):
        for l in range(levels):
            for side, (to, peer, got, buf) in enumerate(sides(l)):
                @pl.when(to)
                def _():
                    send(c, l, side, peer, buf).wait_send()

                @pl.when(got)
                def _():
                    forward(c, l, side, buf).wait_send()
        share(c).wait_send()


def solution(mesh):
    slices = mesh.shape["dom"]

    def body(right_side, lower_blocks, upper_blocks, final_blocks):
        _, levels, half, width = lower_blocks.shape
        rhs = right_side.shape[2]
        chunks = CHUNKS
        cols = rhs // chunks
        bf = jnp.bfloat16
        any_, vm = pl.BlockSpec(memory_space=pl.ANY), pl.BlockSpec(memory_space=pltpu.VMEM)
        dma = pltpu.SemaphoreType.DMA
        return pl.pallas_call(
            functools.partial(kernel, slices, levels),
            out_shape=jax.ShapeDtypeStruct(right_side.shape, jnp.float32),
            in_specs=[vm, any_, any_, any_],
            out_specs=vm,
            scratch_shapes=[
                pltpu.VMEM((levels, half, width), bf),
                pltpu.VMEM((levels, half, width), bf),
                pltpu.VMEM((half, width), bf),
                pltpu.VMEM((half, rhs), jnp.float32),
                pltpu.VMEM((levels, chunks, half, cols), bf),
                pltpu.VMEM((levels, chunks, width, cols), bf),
                pltpu.VMEM((levels, chunks, width, cols), bf),
                pltpu.VMEM((chunks, width, cols), bf),
                dma((2, levels + 1)),
                dma((2, levels, chunks)),
                dma((2, levels, chunks)),
                dma((2, levels, chunks)),
                dma((2, levels, chunks)),
                dma((chunks,)),
                dma((chunks,)),
            ],
            compiler_params=pltpu.CompilerParams(
                collective_id=0, has_side_effects=True, vmem_limit_bytes=56 * 2**20),
        )(right_side, lower_blocks, upper_blocks, final_blocks)

    in_specs = (
        P("dom", "row", None),
        P("dom", None, "row", None),
        P("dom", None, "row", None),
        P("dom", "row", None),
    )
    return jax.shard_map(body, mesh=mesh, in_specs=in_specs, out_specs=P("dom", "row", None), check_vma=False)
```

```python
import functools

import jax
import jax.numpy as jnp
from jax import lax
from jax.experimental import pallas as pl
from jax.experimental.pallas import tpu as pltpu
from jax.sharding import PartitionSpec as P

MESH = pl.DeviceIdType.MESH
LANES = 128
BLOCK = 256
AHEAD = 2
GATE = (0, 0)


def schedule(chunks, levels):
    return [(step - c, c) for step in range(levels + chunks) for c in range(chunks) if 0 <= step - c <= levels]


def kernel(slices, levels, rs_ref, lo_ref, up_ref, state_ref,
           lo_v, up_v, cur, first, snd, low, high,
           w_sem, w_send, w_recv, x_sem, x_send, x_recv,
           f_send, f_recv, s_sem, r_sem, l_sem, o_send, o_recv, gate_sem):
    half = rs_ref.shape[1]
    chunks, width, cols = cur.shape
    me, row = lax.axis_index("dom"), lax.axis_index("row")
    sib = 1 - row
    mine = pl.ds(pl.multiple_of(row * half, half), half)

    barrier = pltpu.get_barrier_semaphore()
    pl.semaphore_signal(barrier, inc=1, device_id=(me, sib), device_id_type=MESH)
    count = 1
    for l in reversed(range(levels)):
        d = 2 ** l
        for ok, peer in ((me >= d, me - d), (me + d < slices, me + d)):
            count = count + (2 if l == 0 else 1) * ok.astype(jnp.int32)

            @pl.when(ok)
            def _():
                pl.semaphore_signal(barrier, inc=1, device_id=(peer, row), device_id_type=MESH)
                if l == 0:
                    pl.semaphore_signal(barrier, inc=1, device_id=(peer, sib), device_id_type=MESH)

    def lanes_of(core, c):
        return pl.ds(pl.multiple_of(core * (chunks * cols) + c * cols, cols), cols)

    def weight(l):
        return ((lo_ref.at[0, l], lo_v.at[l, mine]), (up_ref.at[0, l], up_v.at[l, mine]))

    def own_weight(l):
        return [pltpu.make_async_copy(a, b, w_sem.at[i, l]) for i, (a, b) in enumerate(weight(l))]

    def give_weight(l):
        return [pltpu.make_async_remote_copy(a, b, w_send.at[i, l], w_recv.at[i, l], (me, sib), MESH)
                for i, (a, b) in enumerate(weight(l))]

    def own_source(c):
        return pltpu.make_async_copy(rs_ref.at[0, :, lanes_of(row, c)], cur.at[c, mine], x_sem.at[c])

    def give_source(c):
        return pltpu.make_async_remote_copy(
            rs_ref.at[0, :, lanes_of(sib, c)], cur.at[c, mine], x_send.at[c], x_recv.at[c], (me, sib), MESH)

    def sides(l):
        d = 2 ** l
        return ((me + d < slices, me + d, me >= d, low), (me >= d, me - d, me + d < slices, high))

    def send_first(c, side, peer, core, buf):
        return pltpu.make_async_remote_copy(
            first.at[core, c], buf.at[0, c, mine], f_send.at[side, core, c], f_recv.at[side, row, c], (peer, core), MESH)

    def got_first(c, side, core, buf):
        return pltpu.make_async_remote_copy(
            first.at[core, c], buf.at[0, c, pl.ds(core * half, half)], f_send.at[side, core, c], f_recv.at[side, core, c],
            (me, sib), MESH)

    def send(c, l, side, peer, buf):
        return pltpu.make_async_remote_copy(
            snd.at[l, c], buf.at[l, c], s_sem.at[side, l, c], r_sem.at[side, l, c], (peer, row), MESH)

    def keep_state(c):
        return pltpu.make_async_copy(snd.at[levels, c], state_ref.at[:, lanes_of(row, c)], l_sem.at[c])

    def give_state(c):
        return pltpu.make_async_remote_copy(
            snd.at[levels, c], state_ref.at[:, lanes_of(row, c)], o_send.at[c], o_recv.at[c], (me, sib), MESH)

    def got_state(c):
        return pltpu.make_async_remote_copy(
            snd.at[levels, c], state_ref.at[:, lanes_of(sib, c)], o_send.at[c], o_recv.at[c], (me, sib), MESH)

    def open_core(core):
        for c in range(chunks):
            for side, (to, peer, _, buf) in enumerate(sides(0)):
                @pl.when(to)
                def _():
                    send_first(c, side, peer, core, buf).start()

    def do_math(l, c):
        if c == 0:
            for copy in own_weight(l):
                copy.wait()
            for copy in give_weight(l):
                copy.wait_recv()
        if l == 0:
            own_source(c).wait()
            give_source(c).wait_recv()
        for side, (_, _, got, buf) in enumerate(sides(l)):
            weights = (lo_v, up_v)[side]

            @pl.when(got)
            def _():
                if l == 0:
                    for core in range(2):
                        got_first(c, side, core, buf).wait_recv()
                else:
                    send(c, l, side, me, buf).wait_recv()
                for at in range(0, width, BLOCK):
                    cur[c, at:at + BLOCK] += jnp.dot(
                        weights[l, at:at + BLOCK], buf[l, c], preferred_element_type=jnp.float32)

    def do_send(l, c):
        snd[l, c] = cur[c].astype(jnp.bfloat16)
        if l == levels:
            keep_state(c).start()
            give_state(c).start()
            return
        for side, (to, peer, _, buf) in enumerate(sides(l)):
            @pl.when(to)
            def _():
                send(c, l, side, peer, buf).start()

    for c in range(chunks):
        own_source(c).start()
    for l in range(levels):
        for copy in own_weight(l):
            copy.start()
    for core in range(2):
        for c in range(chunks):
            at = (core * chunks + c) * cols
            first[core, c] = rs_ref[0, :, at:at + cols].astype(jnp.bfloat16)
    pl.semaphore_wait(barrier, count)

    open_core(0)
    for c in range(chunks):
        give_source(c).start()
    for l in range(min(AHEAD, levels)):
        for copy in give_weight(l):
            copy.start()

    @pl.when(row == 1)
    def _():
        pl.semaphore_wait(gate_sem, 1)
        open_core(1)

    for l, c in schedule(chunks, levels):
        if l == levels:
            continue
        if c == 0 and l + AHEAD < levels:
            for copy in give_weight(l + AHEAD):
                copy.start()
        do_math(l, c)
        do_send(l + 1, c)
        if GATE == (l, c):
            @pl.when(row == 0)
            def _():
                pl.semaphore_signal(gate_sem, inc=1, device_id=(me, sib), device_id_type=MESH)
                open_core(1)

    for c in range(chunks):
        keep_state(c).wait()
        got_state(c).wait_recv()
    for c in range(chunks):
        give_source(c).wait_send()
        give_state(c).wait_send()
        for l in range(levels):
            for side, (to, peer, _, buf) in enumerate(sides(l)):
                @pl.when(to)
                def _():
                    if l == 0:
                        for core in range(2):
                            send_first(c, side, peer, core, buf).wait_send()
                    else:
                        send(c, l, side, peer, buf).wait_send()
    for l in range(levels):
        for copy in give_weight(l):
            copy.wait_send()


def solution(mesh):
    slices = mesh.shape["dom"]

    def body(right_side, lower_blocks, upper_blocks, final_blocks):
        _, levels, half, width = lower_blocks.shape
        rhs = right_side.shape[2]
        cols = LANES
        chunks = rhs // 2 // cols
        bf, f32 = jnp.bfloat16, jnp.float32
        any_, vm = pl.BlockSpec(memory_space=pl.ANY), pl.BlockSpec(memory_space=pltpu.VMEM)
        dma = pltpu.SemaphoreType.DMA
        state = pl.pallas_call(
            functools.partial(kernel, slices, levels),
            out_shape=jax.ShapeDtypeStruct((width, rhs), bf),
            in_specs=[vm, any_, any_],
            out_specs=vm,
            scratch_shapes=[
                pltpu.VMEM((levels, width, width), bf),
                pltpu.VMEM((levels, width, width), bf),
                pltpu.VMEM((chunks, width, cols), f32),
                pltpu.VMEM((2, chunks, half, cols), bf),
                pltpu.VMEM((levels + 1, chunks, width, cols), bf),
                pltpu.VMEM((levels, chunks, width, cols), bf),
                pltpu.VMEM((levels, chunks, width, cols), bf),
                dma((2, levels)), dma((2, levels)), dma((2, levels)),
                dma((chunks,)), dma((chunks,)), dma((chunks,)),
                dma((2, 2, chunks)), dma((2, 2, chunks)),
                dma((2, levels, chunks)), dma((2, levels, chunks)),
                dma((chunks,)), dma((chunks,)), dma((chunks,)),
                pltpu.SemaphoreType.REGULAR,
            ],
            compiler_params=pltpu.CompilerParams(
                collective_id=0, has_side_effects=True, vmem_limit_bytes=52 * 2**20),
        )(right_side, lower_blocks, upper_blocks)
        return jnp.dot(final_blocks[0], state, preferred_element_type=f32)[None]

    in_specs = (
        P("dom", "row", None),
        P("dom", None, "row", None),
        P("dom", None, "row", None),
        P("dom", "row", None),
    )
    return jax.shard_map(body, mesh=mesh, in_specs=in_specs, out_specs=P("dom", "row", None), check_vma=False)
```

```python
import functools

import jax
import jax.numpy as jnp
from jax import lax
from jax.experimental import pallas as pl
from jax.experimental.pallas import tpu as pltpu
from jax.sharding import PartitionSpec as P

MESH = pl.DeviceIdType.MESH
LANES = 128
BLOCK = 512
AHEAD = 2
GATE = (0, 0)


def schedule(chunks, levels):
    return [(step - c, c) for step in range(levels + chunks) for c in range(chunks) if 0 <= step - c <= levels]


def kernel(slices, levels, rs_ref, lo_ref, up_ref, state_ref,
           src_v, lo_v, up_v, cur, first, snd, low, high,
           src_sem, w_sem, w_send, w_recv, x_sem, x_send, x_recv,
           f_send, f_recv, s_sem, r_sem, l_sem, o_send, o_recv, gate_sem):
    half = rs_ref.shape[1]
    chunks, width, cols = cur.shape
    me, row = lax.axis_index("dom"), lax.axis_index("row")
    sib = 1 - row
    mine = pl.ds(pl.multiple_of(row * half, half), half)

    source = pltpu.make_async_copy(rs_ref.at[0], src_v, src_sem)
    source.start()
    barrier = pltpu.get_barrier_semaphore()
    pl.semaphore_signal(barrier, inc=1, device_id=(me, sib), device_id_type=MESH)
    count = 1
    for l in reversed(range(levels)):
        d = 2 ** l
        for ok, peer in ((me >= d, me - d), (me + d < slices, me + d)):
            count = count + (2 if l == 0 else 1) * ok.astype(jnp.int32)

            @pl.when(ok)
            def _():
                pl.semaphore_signal(barrier, inc=1, device_id=(peer, row), device_id_type=MESH)
                if l == 0:
                    pl.semaphore_signal(barrier, inc=1, device_id=(peer, sib), device_id_type=MESH)

    def lanes_of(core, c):
        return pl.ds(pl.multiple_of(core * (chunks * cols) + c * cols, cols), cols)

    def weight(l):
        return ((lo_ref.at[0, l], lo_v.at[l, mine]), (up_ref.at[0, l], up_v.at[l, mine]))

    def own_weight(l):
        return [pltpu.make_async_copy(a, b, w_sem.at[i, l]) for i, (a, b) in enumerate(weight(l))]

    def give_weight(l):
        return [pltpu.make_async_remote_copy(a, b, w_send.at[i, l], w_recv.at[i, l], (me, sib), MESH)
                for i, (a, b) in enumerate(weight(l))]

    def own_source(c):
        return pltpu.make_async_copy(rs_ref.at[0, :, lanes_of(row, c)], cur.at[c, mine], x_sem.at[c])

    def give_source(c):
        return pltpu.make_async_remote_copy(
            rs_ref.at[0, :, lanes_of(sib, c)], cur.at[c, mine], x_send.at[c], x_recv.at[c], (me, sib), MESH)

    def sides(l):
        d = 2 ** l
        return ((me + d < slices, me + d, me >= d, low), (me >= d, me - d, me + d < slices, high))

    def send_first(c, side, peer, core, buf):
        return pltpu.make_async_remote_copy(
            first.at[core, c], buf.at[0, c, mine], f_send.at[side, core, c], f_recv.at[side, row, c], (peer, core), MESH)

    def got_first(c, side, core, buf):
        return pltpu.make_async_remote_copy(
            first.at[core, c], buf.at[0, c, pl.ds(core * half, half)], f_send.at[side, core, c], f_recv.at[side, core, c],
            (me, sib), MESH)

    def send(c, l, side, peer, buf):
        return pltpu.make_async_remote_copy(
            snd.at[l, c], buf.at[l, c], s_sem.at[side, l, c], r_sem.at[side, l, c], (peer, row), MESH)

    def keep_state(c):
        return pltpu.make_async_copy(snd.at[levels, c], state_ref.at[:, lanes_of(row, c)], l_sem.at[c])

    def give_state(c):
        return pltpu.make_async_remote_copy(
            snd.at[levels, c], state_ref.at[:, lanes_of(row, c)], o_send.at[c], o_recv.at[c], (me, sib), MESH)

    def got_state(c):
        return pltpu.make_async_remote_copy(
            snd.at[levels, c], state_ref.at[:, lanes_of(sib, c)], o_send.at[c], o_recv.at[c], (me, sib), MESH)

    def open_core(core):
        for c in range(chunks):
            for side, (to, peer, _, buf) in enumerate(sides(0)):
                @pl.when(to)
                def _():
                    send_first(c, side, peer, core, buf).start()

    def do_math(l, c):
        if c == 0:
            for copy in own_weight(l):
                copy.wait()
            for copy in give_weight(l):
                copy.wait_recv()
        if l == 0:
            own_source(c).wait()
            give_source(c).wait_recv()
        for side, (_, _, got, buf) in enumerate(sides(l)):
            weights = (lo_v, up_v)[side]

            @pl.when(got)
            def _():
                if l == 0:
                    for core in range(2):
                        got_first(c, side, core, buf).wait_recv()
                else:
                    send(c, l, side, me, buf).wait_recv()
                for at in range(0, width, BLOCK):
                    cur[c, at:at + BLOCK] += jnp.dot(
                        weights[l, at:at + BLOCK], buf[l, c], preferred_element_type=jnp.float32)

    def do_send(l, c):
        snd[l, c] = cur[c].astype(jnp.bfloat16)
        if l == levels:
            keep_state(c).start()
            give_state(c).start()
            return
        for side, (to, peer, _, buf) in enumerate(sides(l)):
            @pl.when(to)
            def _():
                send(c, l, side, peer, buf).start()

    for c in range(chunks):
        own_source(c).start()
    for l in range(levels):
        for copy in own_weight(l):
            copy.start()
    source.wait()
    for core in range(2):
        for c in range(chunks):
            at = (core * chunks + c) * cols
            first[core, c] = src_v[:, at:at + cols].astype(jnp.bfloat16)
    pl.semaphore_wait(barrier, count)

    open_core(0)
    for c in range(chunks):
        give_source(c).start()
    for l in range(min(AHEAD, levels)):
        for copy in give_weight(l):
            copy.start()

    @pl.when(row == 1)
    def _():
        pl.semaphore_wait(gate_sem, 1)
        open_core(1)

    for l, c in schedule(chunks, levels):
        if l == levels:
            continue
        if c == 0 and l + AHEAD < levels:
            for copy in give_weight(l + AHEAD):
                copy.start()
        do_math(l, c)
        do_send(l + 1, c)
        if GATE == (l, c):
            @pl.when(row == 0)
            def _():
                pl.semaphore_signal(gate_sem, inc=1, device_id=(me, sib), device_id_type=MESH)
                open_core(1)

    for c in range(chunks):
        keep_state(c).wait()
        got_state(c).wait_recv()
    for c in range(chunks):
        give_source(c).wait_send()
        give_state(c).wait_send()
        for l in range(levels):
            for side, (to, peer, _, buf) in enumerate(sides(l)):
                @pl.when(to)
                def _():
                    if l == 0:
                        for core in range(2):
                            send_first(c, side, peer, core, buf).wait_send()
                    else:
                        send(c, l, side, peer, buf).wait_send()
    for l in range(levels):
        for copy in give_weight(l):
            copy.wait_send()


def solution(mesh):
    slices = mesh.shape["dom"]

    def body(right_side, lower_blocks, upper_blocks, final_blocks):
        _, levels, half, width = lower_blocks.shape
        rhs = right_side.shape[2]
        cols = LANES
        chunks = rhs // 2 // cols
        bf, f32 = jnp.bfloat16, jnp.float32
        any_, vm = pl.BlockSpec(memory_space=pl.ANY), pl.BlockSpec(memory_space=pltpu.VMEM)
        dma = pltpu.SemaphoreType.DMA
        state = pl.pallas_call(
            functools.partial(kernel, slices, levels),
            out_shape=jax.ShapeDtypeStruct((width, rhs), bf),
            in_specs=[any_, any_, any_],
            out_specs=vm,
            scratch_shapes=[
                pltpu.VMEM((half, rhs), f32),
                pltpu.VMEM((levels, width, width), bf),
                pltpu.VMEM((levels, width, width), bf),
                pltpu.VMEM((chunks, width, cols), f32),
                pltpu.VMEM((2, chunks, half, cols), bf),
                pltpu.VMEM((levels + 1, chunks, width, cols), bf),
                pltpu.VMEM((levels, chunks, width, cols), bf),
                pltpu.VMEM((levels, chunks, width, cols), bf),
                dma,
                dma((2, levels)), dma((2, levels)), dma((2, levels)),
                dma((chunks,)), dma((chunks,)), dma((chunks,)),
                dma((2, 2, chunks)), dma((2, 2, chunks)),
                dma((2, levels, chunks)), dma((2, levels, chunks)),
                dma((chunks,)), dma((chunks,)), dma((chunks,)),
                pltpu.SemaphoreType.REGULAR,
            ],
            compiler_params=pltpu.CompilerParams(
                collective_id=0, has_side_effects=True, vmem_limit_bytes=52 * 2**20),
        )(right_side, lower_blocks, upper_blocks)
        return jnp.dot(final_blocks[0], state, preferred_element_type=f32)[None]

    in_specs = (
        P("dom", "row", None),
        P("dom", None, "row", None),
        P("dom", None, "row", None),
        P("dom", "row", None),
    )
    return jax.shard_map(body, mesh=mesh, in_specs=in_specs, out_specs=P("dom", "row", None), check_vma=False)
```

```python
import functools

import jax
import jax.numpy as jnp
from jax import lax
from jax.experimental import pallas as pl
from jax.experimental.pallas import tpu as pltpu
from jax.experimental.layout import Layout, with_layout_constraint
from jax.sharding import PartitionSpec as P

MESH = pl.DeviceIdType.MESH
LANES = 128
BLOCK = 512
AHEAD = 2
GATE = (0, 0)


def schedule(chunks, levels):
    return [(step - c, c) for step in range(levels + chunks) for c in range(chunks) if 0 <= step - c <= levels]


def kernel(slices, levels, rs_ref, lo_ref, up_ref, state_ref,
           src_v, lo_v, up_v, cur, first, snd, low, high,
           src_sem, w_sem, w_send, w_recv, x_sem, x_send, x_recv,
           f_send, f_recv, s_sem, r_sem, l_sem, o_send, o_recv, gate_sem):
    half = rs_ref.shape[1]
    chunks, width, cols = cur.shape
    me, row = lax.axis_index("dom"), lax.axis_index("row")
    sib = 1 - row
    mine = pl.ds(pl.multiple_of(row * half, half), half)

    source = pltpu.make_async_copy(rs_ref.at[0], src_v, src_sem)
    source.start()
    barrier = pltpu.get_barrier_semaphore()
    pl.semaphore_signal(barrier, inc=1, device_id=(me, sib), device_id_type=MESH)
    count = 1
    for l in reversed(range(levels)):
        d = 2 ** l
        for ok, peer in ((me >= d, me - d), (me + d < slices, me + d)):
            count = count + (2 if l == 0 else 1) * ok.astype(jnp.int32)

            @pl.when(ok)
            def _():
                pl.semaphore_signal(barrier, inc=1, device_id=(peer, row), device_id_type=MESH)
                if l == 0:
                    pl.semaphore_signal(barrier, inc=1, device_id=(peer, sib), device_id_type=MESH)

    def lanes_of(core, c):
        return pl.ds(pl.multiple_of(core * (chunks * cols) + c * cols, cols), cols)

    def weight(l):
        return ((lo_ref.at[0, l], lo_v.at[l, mine]), (up_ref.at[0, l], up_v.at[l, mine]))

    def own_weight(l):
        return [pltpu.make_async_copy(a, b, w_sem.at[i, l]) for i, (a, b) in enumerate(weight(l))]

    def give_weight(l):
        return [pltpu.make_async_remote_copy(a, b, w_send.at[i, l], w_recv.at[i, l], (me, sib), MESH)
                for i, (a, b) in enumerate(weight(l))]

    def own_source(c):
        return pltpu.make_async_copy(rs_ref.at[0, :, lanes_of(row, c)], cur.at[c, mine], x_sem.at[c])

    def give_source(c):
        return pltpu.make_async_remote_copy(
            rs_ref.at[0, :, lanes_of(sib, c)], cur.at[c, mine], x_send.at[c], x_recv.at[c], (me, sib), MESH)

    def sides(l):
        d = 2 ** l
        return ((me + d < slices, me + d, me >= d, low), (me >= d, me - d, me + d < slices, high))

    def send_first(c, side, peer, core, buf):
        return pltpu.make_async_remote_copy(
            first.at[core, c], buf.at[0, c, mine], f_send.at[side, core, c], f_recv.at[side, row, c], (peer, core), MESH)

    def got_first(c, side, core, buf):
        return pltpu.make_async_remote_copy(
            first.at[core, c], buf.at[0, c, pl.ds(core * half, half)], f_send.at[side, core, c], f_recv.at[side, core, c],
            (me, sib), MESH)

    def send(c, l, side, peer, buf):
        return pltpu.make_async_remote_copy(
            snd.at[l, c], buf.at[l, c], s_sem.at[side, l, c], r_sem.at[side, l, c], (peer, row), MESH)

    def keep_state(c):
        return pltpu.make_async_copy(snd.at[levels, c], state_ref.at[:, lanes_of(row, c)], l_sem.at[c])

    def give_state(c):
        return pltpu.make_async_remote_copy(
            snd.at[levels, c], state_ref.at[:, lanes_of(row, c)], o_send.at[c], o_recv.at[c], (me, sib), MESH)

    def got_state(c):
        return pltpu.make_async_remote_copy(
            snd.at[levels, c], state_ref.at[:, lanes_of(sib, c)], o_send.at[c], o_recv.at[c], (me, sib), MESH)

    def open_core(core):
        for c in range(chunks):
            for side, (to, peer, _, buf) in enumerate(sides(0)):
                @pl.when(to)
                def _():
                    send_first(c, side, peer, core, buf).start()

    def do_math(l, c):
        if c == 0:
            for copy in own_weight(l):
                copy.wait()
            for copy in give_weight(l):
                copy.wait_recv()
        if l == 0:
            own_source(c).wait()
            give_source(c).wait_recv()
        for side, (_, _, got, buf) in enumerate(sides(l)):
            weights = (lo_v, up_v)[side]

            @pl.when(got)
            def _():
                if l == 0:
                    for core in range(2):
                        got_first(c, side, core, buf).wait_recv()
                else:
                    send(c, l, side, me, buf).wait_recv()
                for at in range(0, width, BLOCK):
                    cur[c, at:at + BLOCK] += jnp.dot(
                        weights[l, at:at + BLOCK], buf[l, c], preferred_element_type=jnp.float32)

    def do_send(l, c):
        snd[l, c] = cur[c].astype(jnp.bfloat16)
        if l == levels:
            keep_state(c).start()
            give_state(c).start()
            return
        for side, (to, peer, _, buf) in enumerate(sides(l)):
            @pl.when(to)
            def _():
                send(c, l, side, peer, buf).start()

    for c in range(chunks):
        own_source(c).start()
    for l in range(levels):
        for copy in own_weight(l):
            copy.start()
    source.wait()
    for core in range(2):
        for c in range(chunks):
            at = (core * chunks + c) * cols
            first[core, c] = src_v[:, at:at + cols].astype(jnp.bfloat16)
    pl.semaphore_wait(barrier, count)

    open_core(0)
    for c in range(chunks):
        give_source(c).start()
    for l in range(min(AHEAD, levels)):
        for copy in give_weight(l):
            copy.start()

    @pl.when(row == 1)
    def _():
        pl.semaphore_wait(gate_sem, 1)
        open_core(1)

    for l, c in schedule(chunks, levels):
        if l == levels:
            continue
        if c == 0 and l + AHEAD < levels:
            for copy in give_weight(l + AHEAD):
                copy.start()
        do_math(l, c)
        do_send(l + 1, c)
        if GATE == (l, c):
            @pl.when(row == 0)
            def _():
                pl.semaphore_signal(gate_sem, inc=1, device_id=(me, sib), device_id_type=MESH)
                open_core(1)

    for c in range(chunks):
        keep_state(c).wait()
        got_state(c).wait_recv()
    for c in range(chunks):
        give_source(c).wait_send()
        give_state(c).wait_send()
        for l in range(levels):
            for side, (to, peer, _, buf) in enumerate(sides(l)):
                @pl.when(to)
                def _():
                    if l == 0:
                        for core in range(2):
                            send_first(c, side, peer, core, buf).wait_send()
                    else:
                        send(c, l, side, peer, buf).wait_send()
    for l in range(levels):
        for copy in give_weight(l):
            copy.wait_send()


def solution(mesh):
    slices = mesh.shape["dom"]

    def body(right_side, lower_blocks, upper_blocks, final_blocks):
        _, levels, half, width = lower_blocks.shape
        rhs = right_side.shape[2]
        cols = LANES
        chunks = rhs // 2 // cols
        bf, f32 = jnp.bfloat16, jnp.float32
        any_, vm = pl.BlockSpec(memory_space=pl.ANY), pl.BlockSpec(memory_space=pltpu.VMEM)
        dma = pltpu.SemaphoreType.DMA
        state = pl.pallas_call(
            functools.partial(kernel, slices, levels),
            out_shape=jax.ShapeDtypeStruct((width, rhs), bf),
            in_specs=[any_, any_, any_],
            out_specs=vm,
            scratch_shapes=[
                pltpu.VMEM((half, rhs), f32),
                pltpu.VMEM((levels, width, width), bf),
                pltpu.VMEM((levels, width, width), bf),
                pltpu.VMEM((chunks, width, cols), f32),
                pltpu.VMEM((2, chunks, half, cols), bf),
                pltpu.VMEM((levels + 1, chunks, width, cols), bf),
                pltpu.VMEM((levels, chunks, width, cols), bf),
                pltpu.VMEM((levels, chunks, width, cols), bf),
                dma,
                dma((2, levels)), dma((2, levels)), dma((2, levels)),
                dma((chunks,)), dma((chunks,)), dma((chunks,)),
                dma((2, 2, chunks)), dma((2, 2, chunks)),
                dma((2, levels, chunks)), dma((2, levels, chunks)),
                dma((chunks,)), dma((chunks,)), dma((chunks,)),
                pltpu.SemaphoreType.REGULAR,
            ],
            compiler_params=pltpu.CompilerParams(
                collective_id=0, has_side_effects=True, vmem_limit_bytes=52 * 2**20),
        )(right_side, lower_blocks, upper_blocks)
        product = jnp.dot(final_blocks[0], state, preferred_element_type=f32)
        return with_layout_constraint(product, Layout(major_to_minor=(0, 1)))[None]

    in_specs = (
        P("dom", "row", None),
        P("dom", None, "row", None),
        P("dom", None, "row", None),
        P("dom", "row", None),
    )
    return jax.shard_map(body, mesh=mesh, in_specs=in_specs, out_specs=P("dom", "row", None), check_vma=False)
```

```python
import functools

import jax
import jax.numpy as jnp
from jax import lax
from jax.experimental import pallas as pl
from jax.experimental.pallas import tpu as pltpu
from jax.experimental.layout import Layout, with_layout_constraint
from jax.sharding import PartitionSpec as P

MESH = pl.DeviceIdType.MESH
LANES = 128
BLOCK = 512
AHEAD = 2
GATE = (0, 0)


def schedule(chunks, levels):
    return [(step - c, c) for step in range(levels + chunks) for c in range(chunks) if 0 <= step - c <= levels]


def kernel(slices, levels, rs_ref, lo_ref, up_ref, state_ref,
           src_v, lo_v, up_v, cur, first, snd, low, high,
           src_sem, w_sem, w_send, w_recv, x_sem, x_send, x_recv,
           f_send, f_recv, s_sem, r_sem, l_sem, o_send, o_recv, gate_sem):
    half = rs_ref.shape[1]
    chunks, width, cols = cur.shape
    me, row = lax.axis_index("dom"), lax.axis_index("row")
    sib = 1 - row
    mine = pl.ds(pl.multiple_of(row * half, half), half)

    source = pltpu.make_async_copy(rs_ref.at[0], src_v, src_sem)
    source.start()
    barrier = pltpu.get_barrier_semaphore()
    pl.semaphore_signal(barrier, inc=1, device_id=(me, sib), device_id_type=MESH)
    count = 1
    for l in reversed(range(levels)):
        d = 2 ** l
        for ok, peer in ((me >= d, me - d), (me + d < slices, me + d)):
            count = count + (2 if l == 0 else 1) * ok.astype(jnp.int32)

            @pl.when(ok)
            def _():
                pl.semaphore_signal(barrier, inc=1, device_id=(peer, row), device_id_type=MESH)
                if l == 0:
                    pl.semaphore_signal(barrier, inc=1, device_id=(peer, sib), device_id_type=MESH)

    def lanes_of(core, c):
        return pl.ds(pl.multiple_of(core * (chunks * cols) + c * cols, cols), cols)

    def weight(l):
        return ((lo_ref.at[0, l], lo_v.at[l, mine]), (up_ref.at[0, l], up_v.at[l, mine]))

    def own_weight(l):
        return [pltpu.make_async_copy(a, b, w_sem.at[i, l]) for i, (a, b) in enumerate(weight(l))]

    def give_weight(l):
        return [pltpu.make_async_remote_copy(a, b, w_send.at[i, l], w_recv.at[i, l], (me, sib), MESH)
                for i, (a, b) in enumerate(weight(l))]

    def own_source(c):
        return pltpu.make_async_copy(rs_ref.at[0, :, lanes_of(row, c)], cur.at[c, mine], x_sem.at[c])

    def give_source(c):
        return pltpu.make_async_remote_copy(
            rs_ref.at[0, :, lanes_of(sib, c)], cur.at[c, mine], x_send.at[c], x_recv.at[c], (me, sib), MESH)

    def sides(l):
        d = 2 ** l
        return ((me + d < slices, me + d, me >= d, low), (me >= d, me - d, me + d < slices, high))

    def send_first(c, side, peer, core, buf):
        return pltpu.make_async_remote_copy(
            first.at[core, c], buf.at[0, c, mine], f_send.at[side, core, c], f_recv.at[side, row, c], (peer, core), MESH)

    def got_first(c, side, core, buf):
        return pltpu.make_async_remote_copy(
            first.at[core, c], buf.at[0, c, pl.ds(core * half, half)], f_send.at[side, core, c], f_recv.at[side, core, c],
            (me, sib), MESH)

    def send(c, l, side, peer, buf):
        return pltpu.make_async_remote_copy(
            snd.at[l, c], buf.at[l, c], s_sem.at[side, l, c], r_sem.at[side, l, c], (peer, row), MESH)

    def keep_state(c):
        return pltpu.make_async_copy(snd.at[levels, c], state_ref.at[:, lanes_of(row, c)], l_sem.at[c])

    def give_state(c):
        return pltpu.make_async_remote_copy(
            snd.at[levels, c], state_ref.at[:, lanes_of(row, c)], o_send.at[c], o_recv.at[c], (me, sib), MESH)

    def got_state(c):
        return pltpu.make_async_remote_copy(
            snd.at[levels, c], state_ref.at[:, lanes_of(sib, c)], o_send.at[c], o_recv.at[c], (me, sib), MESH)

    def open_core(core):
        for c in range(chunks):
            for side, (to, peer, _, buf) in enumerate(sides(0)):
                @pl.when(to)
                def _():
                    send_first(c, side, peer, core, buf).start()

    def do_math(l, c):
        if c == 0:
            for copy in own_weight(l):
                copy.wait()
            for copy in give_weight(l):
                copy.wait_recv()
        if l == 0:
            own_source(c).wait()
            give_source(c).wait_recv()
        for side, (_, _, got, buf) in tuple(enumerate(sides(l)))[::-1 if l in (1, 3) else 1]:
            weights = (lo_v, up_v)[side]

            @pl.when(got)
            def _():
                if l == 0:
                    for core in range(2):
                        got_first(c, side, core, buf).wait_recv()
                else:
                    send(c, l, side, me, buf).wait_recv()
                for at in range(0, width, BLOCK):
                    cur[c, at:at + BLOCK] += jnp.dot(
                        weights[l, at:at + BLOCK], buf[l, c], preferred_element_type=jnp.float32)

    def do_send(l, c):
        snd[l, c] = cur[c].astype(jnp.bfloat16)
        if l == levels:
            keep_state(c).start()
            give_state(c).start()
            return
        for side, (to, peer, _, buf) in tuple(enumerate(sides(l)))[::-1 if l in (1, 3) else 1]:
            @pl.when(to)
            def _():
                send(c, l, side, peer, buf).start()

    for c in range(chunks):
        own_source(c).start()
    for l in range(levels):
        for copy in own_weight(l):
            copy.start()
    source.wait()
    for core in range(2):
        for c in range(chunks):
            at = (core * chunks + c) * cols
            first[core, c] = src_v[:, at:at + cols].astype(jnp.bfloat16)
    pl.semaphore_wait(barrier, count)

    open_core(0)
    for c in range(chunks):
        give_source(c).start()
    for l in range(min(AHEAD, levels)):
        for copy in give_weight(l):
            copy.start()

    @pl.when(row == 1)
    def _():
        pl.semaphore_wait(gate_sem, 1)
        open_core(1)

    for l, c in schedule(chunks, levels):
        if l == levels:
            continue
        if c == 0 and l + AHEAD < levels:
            for copy in give_weight(l + AHEAD):
                copy.start()
        do_math(l, c)
        do_send(l + 1, c)
        if GATE == (l, c):
            @pl.when(row == 0)
            def _():
                pl.semaphore_signal(gate_sem, inc=1, device_id=(me, sib), device_id_type=MESH)
                open_core(1)

    for c in range(chunks):
        keep_state(c).wait()
        got_state(c).wait_recv()
    for c in range(chunks):
        give_source(c).wait_send()
        give_state(c).wait_send()
        for l in range(levels):
            for side, (to, peer, _, buf) in enumerate(sides(l)):
                @pl.when(to)
                def _():
                    if l == 0:
                        for core in range(2):
                            send_first(c, side, peer, core, buf).wait_send()
                    else:
                        send(c, l, side, peer, buf).wait_send()
    for l in range(levels):
        for copy in give_weight(l):
            copy.wait_send()


def solution(mesh):
    slices = mesh.shape["dom"]

    def body(right_side, lower_blocks, upper_blocks, final_blocks):
        _, levels, half, width = lower_blocks.shape
        rhs = right_side.shape[2]
        cols = LANES
        chunks = rhs // 2 // cols
        bf, f32 = jnp.bfloat16, jnp.float32
        any_, vm = pl.BlockSpec(memory_space=pl.ANY), pl.BlockSpec(memory_space=pltpu.VMEM)
        dma = pltpu.SemaphoreType.DMA
        state = pl.pallas_call(
            functools.partial(kernel, slices, levels),
            out_shape=jax.ShapeDtypeStruct((width, rhs), bf),
            in_specs=[any_, any_, any_],
            out_specs=vm,
            scratch_shapes=[
                pltpu.VMEM((half, rhs), f32),
                pltpu.VMEM((levels, width, width), bf),
                pltpu.VMEM((levels, width, width), bf),
                pltpu.VMEM((chunks, width, cols), f32),
                pltpu.VMEM((2, chunks, half, cols), bf),
                pltpu.VMEM((levels + 1, chunks, width, cols), bf),
                pltpu.VMEM((levels, chunks, width, cols), bf),
                pltpu.VMEM((levels, chunks, width, cols), bf),
                dma,
                dma((2, levels)), dma((2, levels)), dma((2, levels)),
                dma((chunks,)), dma((chunks,)), dma((chunks,)),
                dma((2, 2, chunks)), dma((2, 2, chunks)),
                dma((2, levels, chunks)), dma((2, levels, chunks)),
                dma((chunks,)), dma((chunks,)), dma((chunks,)),
                pltpu.SemaphoreType.REGULAR,
            ],
            compiler_params=pltpu.CompilerParams(
                collective_id=0, has_side_effects=True, vmem_limit_bytes=52 * 2**20),
        )(right_side, lower_blocks, upper_blocks)
        product = jnp.dot(final_blocks[0], state, preferred_element_type=f32)
        return with_layout_constraint(product, Layout(major_to_minor=(0, 1)))[None]

    in_specs = (
        P("dom", "row", None),
        P("dom", None, "row", None),
        P("dom", None, "row", None),
        P("dom", "row", None),
    )
    return jax.shard_map(body, mesh=mesh, in_specs=in_specs, out_specs=P("dom", "row", None), check_vma=False)
```
